128 devices in a mesh: row: 8 (over z, core), col: 16 (over x, y).
Axes of the slice: x: 4, y: 4, z: 4, core: 2. Of those that a mesh axis runs over, the one named last changes fastest.
Arguments:
- object_slices: bfloat16 [2, 2, 16384, 4096], P(None, None, 'row', 'col'), may hold values from -4 to 4
- probe: float32 [2, 256, 256], replicated, may hold values from -6 to 6
- positions: int32 [2048, 2], P(('row', 'col')), may hold values from 0 to 16128, as said below
- counts: int32 [128], P(('row', 'col')), may hold values from 2 to 16, as said below
- amplitude: bfloat16 [2048, 256, 256], P(('row', 'col')), may hold values from 0.099609375 to 3
Outputs:
- gradient: float32 [2, 2, 16384, 4096], P(None, None, 'row', 'col')
The draws below stay inside these ranges and needn't reach their ends.
Inputs may be any that keep to these rules, and one draw needn't show every extreme that they name: The 16 positions of a device (rows p with p // 16 equal to its index over row+col, row slowest) have their corner inside that device's tile of 2048 x 256, and every window lies inside the object. `counts`: some device has all 16 slots live in every draw.
All inputs are finite; a program needn't handle non-finite values.
Results may differ from the reference program's by a relative error of at most 0.012.
Values may be sent and summed in bfloat16 or wider, within the bound.
No kernel may reach another device: no remote copies, remote signals or barrier semaphores. Data moves between devices by JAX's collectives and lax.ppermute only.
A program may use at most 128 MiB of HBM per device.

```python
import math
import jax
import jax.numpy as jnp
from jax import lax

W = 256
S = 2
SLOTS = 16
TR = 2048
TC = 256
OBJ_H = 16384
OBJ_W = 4096
TILES = 128


def draw_positions(key, part):
    key = jax.random.fold_in(key, 11)
    total = TILES * SLOTS
    slot = jnp.arange(total, dtype=jnp.int32)
    device = slot // SLOTS
    tile_cols = OBJ_W // TC
    row_start = device // tile_cols * TR
    col_start = device % tile_cols * TC
    span_rows = jnp.minimum(TR, OBJ_H - W - row_start + 1)
    span_cols = jnp.minimum(TC, OBJ_W - W - col_start + 1)
    raw = jax.random.randint(key, (total, 2), 0, 1 << 20, dtype=jnp.int32)
    top = row_start + raw[:, 0] % span_rows
    left = col_start + raw[:, 1] % span_cols
    return jnp.stack([top, left], axis=1).astype(jnp.int32)


def draw_counts(key, part):
    key = jax.random.fold_in(key, 23)
    first, second = jax.random.split(key)
    base = jax.random.randint(first, (TILES,), 2, SLOTS // 2 + 1, dtype=jnp.int32)
    busiest = jax.random.randint(second, (), 0, TILES, dtype=jnp.int32)
    return jnp.where(jnp.arange(TILES, dtype=jnp.int32) == busiest, SLOTS, base).astype(jnp.int32)


def levels(rng, dims, cuts, low, largest):
    loudness, own = 1.0, jax.random.fold_in(rng, 6)
    for axis_at, parts in cuts:
        draws = jnp.exp(jax.random.uniform(jax.random.fold_in(own, axis_at), (parts,), jnp.float32, low / len(cuts), largest / len(cuts)))
        loudness = loudness * jnp.repeat(draws, dims[axis_at] // parts).reshape([-1 if axis == axis_at else 1 for axis in range(len(dims))])
    return loudness


def gaussian(own_key, extent, spread, most, cuts=(), kind=jnp.bfloat16):
    array = jax.random.normal(own_key, extent, jnp.float32) * spread
    if len(cuts) > 0:
        array = levels(own_key, extent, cuts, -0.22, 0.18) * array
    return jnp.clip(array, min=-most, max=most).astype(kind)


def setup_inputs(seed: int = 0) -> dict:
    streams_of = jax.random.split(jax.random.key(seed), 6)
    object_slices = gaussian(streams_of[0], (S, 2, OBJ_H, OBJ_W), 0.7, 4.0, ((2, 8), (3, 16)))
    probe = gaussian(streams_of[1], (2, W, W), 1.0, 6.0, (), jnp.float32)
    positions = draw_positions(jax.random.fold_in(streams_of[5], 71), 0)
    counts = draw_counts(jax.random.fold_in(streams_of[5], 71), 0)
    amplitude = jnp.clip(jnp.exp(math.log(3.0) - 3.4051113 * jax.random.uniform(streams_of[4], (TILES * SLOTS, W, W), jnp.float32) ** levels(streams_of[4], (TILES * SLOTS, W, W), ((0, 128),), -0.2, 0.2)), 0.099609375, 3.0).astype(jnp.bfloat16)
    return dict(object_slices=object_slices, probe=probe, positions=positions, counts=counts, amplitude=amplitude)


def tables(width):
    index = jnp.arange(width, dtype=jnp.int32)
    product = index[:, None] * index[None, :] % width
    angle = product.astype(jnp.float32) * (-2.0 * math.pi / width)
    norm = 1.0 / math.sqrt(width)
    four_re = jnp.cos(angle) * norm
    four_im = jnp.sin(angle) * norm
    freq = ((index + width // 2) % width - width // 2).astype(jnp.float32)
    phase = freq * freq * (-math.pi / (4.0 * width))
    chirp_re = jnp.cos(phase)
    chirp_im = jnp.sin(phase)
    left_re = four_re * chirp_re[None, :] + four_im * chirp_im[None, :]
    left_im = four_re * chirp_im[None, :] - four_im * chirp_re[None, :]
    high = lax.Precision.HIGHEST
    prop_re = jnp.dot(left_re, four_re, precision=high) - jnp.dot(left_im, four_im, precision=high)
    prop_im = jnp.dot(left_re, four_im, precision=high) + jnp.dot(left_im, four_re, precision=high)
    return (four_re.astype(jnp.bfloat16), four_im.astype(jnp.bfloat16), prop_re.astype(jnp.bfloat16), prop_im.astype(jnp.bfloat16))

def transform(mat_re, mat_im, field_re, field_im):
    real_b = field_re.astype(jnp.bfloat16)
    imag_b = field_im.astype(jnp.bfloat16)
    f32 = jnp.float32
    half_re = (jnp.dot(mat_re, real_b, preferred_element_type=f32) - jnp.dot(mat_im, imag_b, preferred_element_type=f32)).astype(jnp.bfloat16)
    half_im = (jnp.dot(mat_re, imag_b, preferred_element_type=f32) + jnp.dot(mat_im, real_b, preferred_element_type=f32)).astype(jnp.bfloat16)
    out_re = jnp.dot(half_re, mat_re, preferred_element_type=f32) - jnp.dot(half_im, mat_im, preferred_element_type=f32)
    out_im = jnp.dot(half_re, mat_im, preferred_element_type=f32) + jnp.dot(half_im, mat_re, preferred_element_type=f32)
    return (out_re, out_im)

def window_gradient(window, measured, alive, probe, tabs):
    four_re, four_im, prop_re, prop_im = tabs
    depth = window.shape[0]

    def compute(operands):
        window, measured, probe = operands
        field_re = probe[0]
        field_im = probe[1]
        entering = []
        slice_re = []
        slice_im = []
        for layer in range(depth):
            entering.append((field_re, field_im))
            obj_re = window[layer, 0].astype(jnp.float32)
            obj_im = window[layer, 1].astype(jnp.float32)
            slice_re.append(obj_re)
            slice_im.append(obj_im)
            exit_re = field_re * obj_re - field_im * obj_im
            exit_im = field_re * obj_im + field_im * obj_re
            if layer < depth - 1:
                field_re, field_im = transform(prop_re, prop_im, exit_re, exit_im)
        far_re, far_im = transform(four_re, four_im, exit_re, exit_im)
        factor = 1.0 - measured.astype(jnp.float32) * lax.rsqrt(far_re * far_re + far_im * far_im + 1.0)
        back_re, back_im = transform(four_re, -four_im, far_re * factor, far_im * factor)
        grads = [None] * depth
        for layer in range(depth - 1, -1, -1):
            in_re, in_im = entering[layer]
            grads[layer] = jnp.stack([in_re * back_re + in_im * back_im, in_re * back_im - in_im * back_re])
            if layer > 0:
                obj_re = slice_re[layer]
                obj_im = slice_im[layer]
                next_re = back_re * obj_re + back_im * obj_im
                next_im = back_im * obj_re - back_re * obj_im
                back_re, back_im = transform(prop_re, -prop_im, next_re, next_im)
        return jnp.stack(grads)

    def skip(operands):
        window = operands[0]
        return jnp.zeros(window.shape, jnp.float32)
    return lax.cond(alive > 0, compute, skip, (window, measured, probe))

def reference(object_slices, probe, positions, counts, amplitude):
    tabs = tables(W)
    zero = jnp.zeros((), jnp.int32)
    total = jnp.zeros((S, 2, OBJ_H, OBJ_W), jnp.float32)

    def step(slot, acc):
        slot = slot.astype(jnp.int32)
        alive = (slot % SLOTS < counts[slot // SLOTS]).astype(jnp.int32)
        top = positions[slot, 0].astype(jnp.int32)
        left = positions[slot, 1].astype(jnp.int32)
        window = lax.dynamic_slice(object_slices, (zero, zero, top, left), (S, 2, W, W))
        measured = lax.dynamic_index_in_dim(amplitude, slot, 0, keepdims=False)
        grads = window_gradient(window, measured, alive, probe, tabs)
        current = lax.dynamic_slice(acc, (zero, zero, top, left), (S, 2, W, W))
        return lax.dynamic_update_slice(acc, current + grads, (zero, zero, top, left))
    return lax.fori_loop(0, TILES * SLOTS, step, total)
```

```python
import functools
import math

import jax
import jax.numpy as jnp
import numpy as np
from jax import lax
from jax.experimental import pallas as pl
from jax.experimental.pallas import tpu as pltpu
from jax.sharding import PartitionSpec as P

W = 256
S = 2
SLOTS = 16
TR = 2048
TC = 256
PLANES = 2 * S
BF16 = jnp.bfloat16
F32 = jnp.float32
CUTS = (2048, 1664, 1408, 1152, 896, 640, 384, 128, 0)


def shifted(value, moves):
    rows, cols = lax.axis_size("row"), lax.axis_size("col")
    pairs = [
        (r * cols + c, (r + moves[0]) * cols + c + moves[1])
        for r in range(rows)
        for c in range(cols)
        if 0 <= r + moves[0] < rows and 0 <= c + moves[1] < cols
    ]
    return lax.ppermute(value, ("row", "col"), pairs)


def tables(width):
    index = np.arange(width)
    four = np.exp(-2j * np.pi * (index[:, None] * index[None, :] % width) / width) / math.sqrt(width)
    freq = (index + width // 2) % width - width // 2
    prop = (four.conj() * np.exp(-1j * np.pi * freq * freq / (4.0 * width))) @ four
    forms = []
    for table in (prop, four):
        re, im = table.real.astype(np.float32), table.imag.astype(np.float32)
        forms.append(np.block([[re, -im], [im, re]]))
        forms.append(np.block([[re, im], [-im, re]]))
    return np.stack(forms).astype(BF16)


def transform(left, right, re, im):
    field = jnp.concatenate([re.astype(BF16), im.astype(BF16)], axis=0)
    half = jnp.dot(left, field, preferred_element_type=F32).astype(BF16)
    half = jnp.concatenate([half[:W], half[W:]], axis=1)
    out = jnp.dot(half, right, preferred_element_type=F32)
    return out[:, :W], out[:, W:]


def window_gradients(windows, amps, probes, tabs):
    many = range(len(amps))
    q_l, q_r, f_l, f_r = (tabs[i] for i in range(4))
    exits = [
        (p[0] * w[0] - p[1] * w[1], p[0] * w[1] + p[1] * w[0]) for p, w in zip(probes, windows)
    ]
    entering = [transform(q_l, q_r, *exits[i]) for i in many]
    exits = [
        (e[0] * w[2] - e[1] * w[3], e[0] * w[3] + e[1] * w[2]) for e, w in zip(entering, windows)
    ]
    fars = [transform(f_l, f_r, *exits[i]) for i in many]
    factors = [
        1.0 - amps[i] * lax.rsqrt(fars[i][0] * fars[i][0] + fars[i][1] * fars[i][1] + 1.0) for i in many
    ]
    backs = [transform(f_r, f_l, fars[i][0] * factors[i], fars[i][1] * factors[i]) for i in many]
    second = [
        (e[0] * b[0] + e[1] * b[1], e[0] * b[1] - e[1] * b[0]) for e, b in zip(entering, backs)
    ]
    nexts = [
        (b[0] * w[2] + b[1] * w[3], b[1] * w[2] - b[0] * w[3]) for b, w in zip(backs, windows)
    ]
    backs = [transform(q_r, q_l, *nexts[i]) for i in many]
    first = [
        (p[0] * b[0] + p[1] * b[1], p[0] * b[1] - p[1] * b[0]) for p, b in zip(probes, backs)
    ]
    return [first[i] + second[i] for i in many]


def range_kernel(low, high, mine_parts, right_parts, *refs):
    refs = list(refs)
    span = high - low
    first, last = high == TR, low == 0
    take = refs.pop
    place_ref, probe_ref, tab_ref, amp_ref = (take(0) for _ in range(4))
    drop_ref = take(0) if last else None
    carry_ref = None if first else take(0)
    mine_refs = [take(0) for _ in range(1 + max(part[0] for part in mine_parts))]
    right_refs = [take(0) for _ in range(1 + max(part[0] for part in right_parts))]
    main_ref, spill_ref = take(0), take(0)
    next_ref = None if last else take(0)
    fall_ref = take(0) if first else None
    mine, right, acc, amps, order, amp_sem, sem = refs

    copies = []
    for parts, sources, target in ((mine_parts, mine_refs, mine), (right_parts, right_refs, right)):
        for which, start, at, rows in parts:
            copies.append((sources[which].at[:, pl.ds(start, rows)], target.at[:, pl.ds(at, rows)]))
    if not first:
        copies.append((carry_ref, acc.at[:, pl.ds(span, W)]))
    copies = [pltpu.make_async_copy(a, b, sem.at[i]) for i, (a, b) in enumerate(copies)]
    for copy in copies:
        copy.start()

    def amp_copy(slot):
        return pltpu.make_async_copy(amp_ref.at[slot], amps.at[slot], amp_sem.at[slot])

    count = jnp.zeros((), jnp.int32)
    inside = []
    for slot in range(SLOTS):
        top = place_ref[slot, 0]
        here = jnp.logical_and(slot < place_ref[SLOTS, 0], jnp.logical_and(top >= low, top < high))
        inside.append(here)

        @pl.when(here)
        def _(slot=slot, count=count):
            order[count] = slot
            amp_copy(slot).start()

        count = count + here.astype(jnp.int32)

    fresh = span + W if first else span
    acc[:, :fresh] = jnp.zeros((PLANES, fresh, 2 * TC), F32)
    for copy in copies:
        copy.wait()
    if last:
        acc[:, :W] += drop_ref[...].astype(F32)
    for slot in range(SLOTS):

        @pl.when(inside[slot])
        def _(slot=slot):
            amp_copy(slot).wait()

    row = lax.broadcasted_iota(jnp.int32, (W, TC), 0)
    col = lax.broadcasted_iota(jnp.int32, (W, TC), 1)

    def step(pair, _):
        slots, masks, places, windows, probes = [], [], [], [], []
        for which in range(2):
            at = 2 * pair + which
            valid = at < count
            slot = order[jnp.minimum(at, count - 1)]
            top = place_ref[slot, 0] - low
            base = pl.multiple_of(top // W * W, W)
            turn = top - base
            edge = place_ref[slot, 1]
            below, beside = row >= turn, col >= edge
            near, far = pl.ds(base, W), pl.ds(base + W, W)
            window = []
            for plane in range(PLANES):
                one = jnp.where(below, mine[plane, near].astype(F32), mine[plane, far].astype(F32))
                two = jnp.where(below, right[plane, near].astype(F32), right[plane, far].astype(F32))
                window.append(jnp.where(beside, one, two))
            probes.append(
                [pltpu.roll(pltpu.roll(probe_ref[part], turn, 0), edge, 1) for part in range(2)]
            )
            windows.append(window)
            slots.append(slot)
            masks.append((row >= jnp.where(valid, turn, W), row < jnp.where(valid, turn, 0), beside))
            places.append((near, far))
        grads = window_gradients(windows, [amps[s].astype(F32) for s in slots], probes, tab_ref)
        for grad, mask, place in zip(grads, masks, places):
            for plane in range(PLANES):
                for half in range(2):
                    part = jnp.where(mask[half], grad[plane], 0.0)
                    left = jnp.where(mask[2], part, 0.0)
                    acc[plane, place[half], :TC] += left
                    acc[plane, place[half], TC:] += part - left
        return 0

    lax.fori_loop(0, (count + 1) // 2, step, 0)
    begin = 0 if last else W
    end = span if first else span + W
    results = [(acc.at[:, pl.ds(begin, end - begin), pl.ds(0, TC)], main_ref)]
    if not last:
        results.append((acc.at[:, pl.ds(0, W)], next_ref))
    results = [pltpu.make_async_copy(a, b, sem.at[i]) for i, (a, b) in enumerate(results)]
    for copy in results:
        copy.start()
    spill_ref[...] = acc[:, begin:end, TC:].astype(BF16)
    if first:
        fall_ref[...] = acc[:, span:, :][:, :W].astype(BF16)
    for copy in results:
        copy.wait()


def parts_of(low, high, pieces):
    used = [i for i, (a, b) in enumerate(pieces) if max(a, low) < min(b, high)]
    parts = []
    for which, i in enumerate(used):
        a, b = max(pieces[i][0], low), min(pieces[i][1], high)
        parts.append((which, a - pieces[i][0], a - low, b - a))
    return used, parts


def range_gradients(low, high, place, probe, tabs, amplitude, drop, carry, mine, rights):
    span = high - low
    first, last = high == TR, low == 0
    top = -(-span // W) * W + W
    spans = [[(at, at + array.shape[1]) for at, array in side] for side in (mine, rights)]
    mine_used, mine_parts = parts_of(low, high + W, spans[0])
    right_used, right_parts = parts_of(low, high + W, spans[1])
    anywhere = pl.BlockSpec(memory_space=pl.ANY)
    vmem = pl.BlockSpec(memory_space=pltpu.VMEM)
    args = [(place, pl.BlockSpec(memory_space=pltpu.SMEM)), (probe, vmem), (tabs, vmem), (amplitude, anywhere)]
    if last:
        args.append((drop, vmem))
    if not first:
        args.append((carry, anywhere))
    args += [(mine[i][1], anywhere) for i in mine_used]
    args += [(rights[i][1], anywhere) for i in right_used]
    final = span + W * (int(last) - int(first))
    outs = [((PLANES, final, TC), F32, anywhere), ((PLANES, final, TC), BF16, vmem)]
    if not last:
        outs.append(((PLANES, W, 2 * TC), F32, anywhere))
    if first:
        outs.append(((PLANES, W, 2 * TC), BF16, vmem))
    return pl.pallas_call(
        functools.partial(range_kernel, low, high, mine_parts, right_parts),
        out_shape=[jax.ShapeDtypeStruct(shape, kind) for shape, kind, _ in outs],
        in_specs=[spec for _, spec in args],
        out_specs=[spec for _, _, spec in outs],
        scratch_shapes=[
            pltpu.VMEM((PLANES, top, TC), BF16),
            pltpu.VMEM((PLANES, top, TC), BF16),
            pltpu.VMEM((PLANES, top, 2 * TC), F32),
            pltpu.VMEM((SLOTS, W, W), BF16),
            pltpu.SMEM((SLOTS,), jnp.int32),
            pltpu.SemaphoreType.DMA((SLOTS,)),
            pltpu.SemaphoreType.DMA((8,)),
        ],
        compiler_params=pltpu.CompilerParams(vmem_limit_bytes=40 << 20),
        cost_estimate=pl.CostEstimate(flops=3 << 30, bytes_accessed=12 << 20, transcendentals=1 << 17),
    )(*[array for array, _ in args])


def body(object_slices, probe, positions, counts, amplitude):
    tabs = jnp.asarray(tables(W))
    obj = object_slices.reshape(PLANES, TR, TC)
    top = positions[:, 0] - lax.axis_index("row") * TR
    left = positions[:, 1] - lax.axis_index("col") * TC
    place = jnp.stack([jnp.append(top, counts[0]), jnp.append(left, counts[0])], axis=1)
    head = obj[:, :W]
    rights = [(TR, shifted(head, (-1, -1)))]
    mine = [(TR, shifted(head, (-1, 0))), (0, obj)]
    ranges = list(zip(CUTS[1:], CUTS[:-1]))
    for low, high in ranges:
        rights.append((low, shifted(obj[:, low:high], (0, -1))))
    total = jnp.zeros((PLANES, TR, TC), F32)
    carry = drop = None
    parts = []
    for low, high in ranges:
        outs = list(
            range_gradients(low, high, place, probe, tabs, amplitude, drop, carry, mine, rights)
        )
        main, spill = outs[:2]
        carry = outs[2] if low > 0 else None
        if high == TR:
            drop = shifted(outs[3], (1, 0))
        begin = low + W if low > 0 else 0
        parts.append((begin, main, shifted(spill, (0, 1))))
    for begin, main, spill in parts:
        total = lax.dynamic_update_slice(total, main + spill.astype(F32), (0, begin, 0))
    return total.reshape(S, 2, TR, TC)


def solution(mesh):
    placed = (
        P(None, None, "row", "col"),
        P(),
        P(("row", "col"), None),
        P(("row", "col")),
        P(("row", "col"), None, None),
    )
    return jax.shard_map(
        body, mesh=mesh, in_specs=placed, out_specs=P(None, None, "row", "col"), check_vma=False
    )
```

```python
import functools
import math

import jax
import jax.numpy as jnp
import numpy as np
from jax import lax
from jax.experimental import pallas as pl
from jax.experimental.pallas import tpu as pltpu
from jax.sharding import PartitionSpec as P

W = 256
S = 2
SLOTS = 16
TR = 2048
TC = 256
PLANES = 2 * S
BF16 = jnp.bfloat16
F32 = jnp.float32
CUTS = (2048, 1664, 1408, 1024, 576, 128, 0)
AHEAD = 3
GROUP = 16
LANES = 128


def shifted(value, moves):
    rows, cols = lax.axis_size("row"), lax.axis_size("col")
    pairs = [
        (r * cols + c, (r + moves[0]) * cols + c + moves[1])
        for r in range(rows)
        for c in range(cols)
        if 0 <= r + moves[0] < rows and 0 <= c + moves[1] < cols
    ]
    return lax.ppermute(value, ("row", "col"), pairs)


def tables(width):
    index = np.arange(width)
    four = np.exp(-2j * np.pi * (index[:, None] * index[None, :] % width) / width) / math.sqrt(width)
    freq = (index + width // 2) % width - width // 2
    prop = (four.conj() * np.exp(-1j * np.pi * freq * freq / (4.0 * width))) @ four
    forms = []
    for table in (prop, four):
        re, im = table.real.astype(np.float32), table.imag.astype(np.float32)
        forms.append(np.block([[re, -im], [im, re]]))
        forms.append(np.block([[re, im], [-im, re]]))
    return np.stack(forms).astype(BF16)


def transform(left, right, re, im):
    field = jnp.concatenate([re.astype(BF16), im.astype(BF16)], axis=0)
    half = jnp.dot(left, field, preferred_element_type=F32).astype(BF16)
    half = jnp.concatenate([half[:W], half[W:]], axis=1)
    out = jnp.dot(half, right, preferred_element_type=F32)
    return out[:, :W], out[:, W:]


def window_gradients(windows, amps, probes, tabs, emit):
    many = range(len(amps))
    q_l, q_r, f_l, f_r = (tabs[i] for i in range(4))
    entering, fars, backs, lasts = {}, {}, {}, {}

    def stage(i, k):
        p, w = probes[i], windows[i]
        if k == 0:
            entering[i] = transform(q_l, q_r, p[0] * w[0] - p[1] * w[1], p[0] * w[1] + p[1] * w[0])
        elif k == 1:
            e = entering[i]
            fars[i] = transform(f_l, f_r, e[0] * w[2] - e[1] * w[3], e[0] * w[3] + e[1] * w[2])
        elif k == 2:
            f = fars[i]
            factor = 1.0 - amps[i] * lax.rsqrt(f[0] * f[0] + f[1] * f[1] + 1.0)
            backs[i] = transform(f_r, f_l, f[0] * factor, f[1] * factor)
        elif k == 3:
            b, e = backs[i], entering[i]
            lasts[i] = transform(q_r, q_l, b[0] * w[2] + b[1] * w[3], b[1] * w[2] - b[0] * w[3])
            emit(i, 2, e[0] * b[0] + e[1] * b[1])
            emit(i, 3, e[0] * b[1] - e[1] * b[0])
        else:
            b = lasts[i]
            emit(i, 0, p[0] * b[0] + p[1] * b[1])
            emit(i, 1, p[0] * b[1] - p[1] * b[0])

    for k in range(5):
        for i in many:
            stage(i, k)


def range_kernel(low, high, mine_parts, right_parts, whole, send, *refs):
    refs = list(refs)
    span = high - low
    first, last = high == TR, low == 0
    take = refs.pop
    place_ref, probe_ref, tab_ref, amp_ref = (take(0) for _ in range(4))
    drop_ref = take(0) if last else None
    carry_ref = None if first else take(0)
    mine_refs = [take(0) for _ in range(1 + max(part[0] for part in mine_parts))]
    right_refs = [take(0) for _ in range(1 + max(part[0] for part in right_parts))]
    main_ref, spill_ref = take(0), take(0)
    next_ref = None if last else take(0)
    fall_ref = take(0) if first else None
    send_ref = take(0) if send else None
    mine, right, acc, amps, twice, win, gone, order, amp_sem, sem = refs

    copies = []
    for parts, sources, target in ((mine_parts, mine_refs, mine), (right_parts, right_refs, right)):
        for which, start, at, rows in parts:
            copies.append((sources[which].at[:, pl.ds(start, rows)], target.at[:, pl.ds(at, rows)]))
    if not first:
        copies.append((carry_ref, acc.at[:, pl.ds(span, W)]))
    copies = [pltpu.make_async_copy(a, b, sem.at[i]) for i, (a, b) in enumerate(copies)]
    for copy in copies:
        copy.start()
    if send:
        ahead = pltpu.make_async_copy(mine_refs[whole].at[:, pl.ds(send[0], send[1] - send[0])], send_ref, sem.at[7])
        ahead.start()

    def amp_copy(slot):
        return pltpu.make_async_copy(amp_ref.at[slot], amps.at[slot], amp_sem.at[slot])

    count = jnp.zeros((), jnp.int32)
    inside = []
    for slot in range(SLOTS):
        top = place_ref[slot, 0]
        here = jnp.logical_and(slot < place_ref[SLOTS, 0], jnp.logical_and(top >= low, top < high))
        inside.append(here)

        @pl.when(here)
        def _(slot=slot, count=count):
            order[count] = slot
            amp_copy(slot).start()

        count = count + here.astype(jnp.int32)

    fresh = span + W if first else span
    acc[:, :fresh] = jnp.zeros((PLANES, fresh, 2 * TC), F32)
    for copy in copies:
        copy.wait()
    if last:
        acc[:, :W] += drop_ref[...].astype(F32)
    for slot in range(SLOTS):

        @pl.when(inside[slot])
        def _(slot=slot):
            amp_copy(slot).wait()

    for half in range(TC // LANES):
        for again in range(2):
            twice[:, half, again * W : again * W + W] = probe_ref[:, :, half * LANES : (half + 1) * LANES]
    row = lax.broadcasted_iota(jnp.int32, (GROUP, TC), 0)
    col = lax.broadcasted_iota(jnp.int32, (GROUP, TC), 1)
    row_b, col_b = row.astype(F32).astype(BF16), col.astype(F32).astype(BF16)
    groups = range(W // GROUP)

    def step(pair, _):
        slots, places, windows, probes = [], [], [], []
        for which in range(2):
            at = 2 * pair + which
            slot = order[jnp.minimum(at, count - 1)]
            top = place_ref[slot, 0] - low
            base = top // W * W
            turn = top - base
            edge = place_ref[slot, 1]
            split = turn // GROUP
            rest = turn - split * GROUP
            beside = col_b >= jnp.full((GROUP, TC), edge, jnp.int32).astype(F32).astype(BF16)
            rows = [pl.multiple_of(base + GROUP * i + jnp.where(i < split, W, 0), GROUP) for i in groups]
            near = pl.ds(pl.multiple_of(base + GROUP * split, GROUP), GROUP)
            far = pl.ds(pl.multiple_of(base + GROUP * split + W, GROUP), GROUP)
            cut = pl.ds(pl.multiple_of(GROUP * split, GROUP), GROUP)
            below = row_b >= jnp.full((GROUP, TC), rest, jnp.int32).astype(F32).astype(BF16)
            for plane in range(PLANES):
                for i in groups:
                    part = pl.ds(rows[i], GROUP)
                    win[which, plane, GROUP * i : GROUP * (i + 1)] = jnp.where(
                        beside, mine[plane, part], right[plane, part]
                    )
                one = jnp.where(below, mine[plane, near], mine[plane, far])
                two = jnp.where(below, right[plane, near], right[plane, far])
                win[which, plane, cut] = jnp.where(beside, one, two)
            turned = [
                jnp.concatenate([twice[part, half, pl.ds(W - turn, W)] for half in range(TC // LANES)], axis=1)
                for part in range(2)
            ]
            probes.append([pltpu.roll(part, edge, 1) for part in turned])
            windows.append([win[which, plane].astype(F32) for plane in range(PLANES)])
            slots.append(slot)
            places.append((at < count, split, rest, col >= edge, rows, far, cut))

        def emit(which, plane, grad):
            valid, split, rest, beside, rows, far, cut = places[which]
            gone[which, plane] = grad
            for i in groups:
                first_row = jnp.where(i == split, rest, 0)
                part = grad[GROUP * i : GROUP * (i + 1)]
                part = jnp.where(row >= jnp.where(valid, first_row, GROUP), part, 0.0)
                left = jnp.where(beside, part, 0.0)
                acc[plane, pl.ds(rows[i], GROUP), :TC] += left
                acc[plane, pl.ds(rows[i], GROUP), TC:] += part - left
            part = jnp.where(row < jnp.where(valid, rest, 0), gone[which, plane, cut], 0.0)
            left = jnp.where(beside, part, 0.0)
            acc[plane, far, :TC] += left
            acc[plane, far, TC:] += part - left

        window_gradients(windows, [amps[s].astype(F32) for s in slots], probes, tab_ref, emit)
        return 0

    lax.fori_loop(0, (count + 1) // 2, step, 0)
    begin = 0 if last else W
    end = span if first else span + W
    results = [(acc.at[:, pl.ds(begin, end - begin), pl.ds(0, TC)], main_ref)]
    if not last:
        results.append((acc.at[:, pl.ds(0, W)], next_ref))
    results = [pltpu.make_async_copy(a, b, sem.at[i]) for i, (a, b) in enumerate(results)]
    for copy in results:
        copy.start()
    spill_ref[...] = acc[:, begin:end, TC:].astype(BF16)
    if first:
        fall_ref[...] = acc[:, span : span + W].astype(BF16)
    for copy in results:
        copy.wait()
    if send:
        ahead.wait()


def parts_of(low, high, pieces):
    used = [i for i, (a, b) in enumerate(pieces) if max(a, low) < min(b, high)]
    parts = []
    for which, i in enumerate(used):
        a, b = max(pieces[i][0], low), min(pieces[i][1], high)
        parts.append((which, a - pieces[i][0], a - low, b - a))
    return used, parts


def range_gradients(low, high, place, probe, tabs, amplitude, drop, carry, mine, rights, send):
    span = high - low
    first, last = high == TR, low == 0
    top = -(-span // W) * W + W
    spans = [[(at, at + array.shape[1]) for at, array in side] for side in (mine, rights)]
    mine_used, mine_parts = parts_of(low, high + W, spans[0])
    right_used, right_parts = parts_of(low, high + W, spans[1])
    anywhere = pl.BlockSpec(memory_space=pl.ANY)
    vmem = pl.BlockSpec(memory_space=pltpu.VMEM)
    args = [(place, pl.BlockSpec(memory_space=pltpu.SMEM)), (probe, vmem), (tabs, vmem), (amplitude, pl.BlockSpec(memory_space=pltpu.HBM))]
    if last:
        args.append((drop, vmem))
    if not first:
        args.append((carry, anywhere))
    args += [(mine[i][1], anywhere) for i in mine_used]
    args += [(rights[i][1], anywhere) for i in right_used]
    final = span + W * (int(last) - int(first))
    outs = [((PLANES, final, TC), F32, anywhere), ((PLANES, final, TC), BF16, vmem)]
    if not last:
        outs.append(((PLANES, W, 2 * TC), F32, anywhere))
    if first:
        outs.append(((PLANES, W, 2 * TC), BF16, vmem))
    if send:
        outs.append(((PLANES, send[1] - send[0], TC), BF16, vmem))
    whole = mine_used.index(len(mine) - 1)
    return pl.pallas_call(
        functools.partial(range_kernel, low, high, mine_parts, right_parts, whole, send),
        out_shape=[jax.ShapeDtypeStruct(shape, kind) for shape, kind, _ in outs],
        in_specs=[spec for _, spec in args],
        out_specs=[spec for _, _, spec in outs],
        scratch_shapes=[
            pltpu.VMEM((PLANES, top, TC), BF16),
            pltpu.VMEM((PLANES, top, TC), BF16),
            pltpu.VMEM((PLANES, top, 2 * TC), F32),
            pltpu.VMEM((SLOTS, W, W), BF16),
            pltpu.VMEM((2, TC // LANES, 2 * W, LANES), F32),
            pltpu.VMEM((2, PLANES, W, W), BF16),
            pltpu.VMEM((2, PLANES, W, W), F32),
            pltpu.SMEM((SLOTS,), jnp.int32),
            pltpu.SemaphoreType.DMA((SLOTS,)),
            pltpu.SemaphoreType.DMA((8,)),
        ],
        compiler_params=pltpu.CompilerParams(vmem_limit_bytes=40 << 20),
        cost_estimate=pl.CostEstimate(flops=3 << 30, bytes_accessed=12 << 20, transcendentals=1 << 17),
    )(*[array for array, _ in args])


def first_pieces(obj, rows):
    def kernel(obj_ref, *refs):
        sem = refs[-1]
        copies = [
            pltpu.make_async_copy(obj_ref.at[:, pl.ds(low, high - low)], ref, sem.at[i])
            for i, ((low, high), ref) in enumerate(zip(rows, refs))
        ]
        for copy in copies:
            copy.start()
        for copy in copies:
            copy.wait()

    anywhere = pl.BlockSpec(memory_space=pl.ANY)
    return pl.pallas_call(
        kernel,
        out_shape=[jax.ShapeDtypeStruct((PLANES, high - low, TC), BF16) for low, high in rows]
        + [jax.ShapeDtypeStruct((PLANES, TR, TC), F32)],
        in_specs=[anywhere],
        out_specs=[pl.BlockSpec(memory_space=pltpu.VMEM)] * len(rows) + [pl.BlockSpec(memory_space=pltpu.HBM)],
        scratch_shapes=[pltpu.SemaphoreType.DMA((len(rows),))],
        cost_estimate=pl.CostEstimate(flops=0, bytes_accessed=4 << 20, transcendentals=0),
    )(obj)


def body(object_slices, probe, positions, counts, amplitude):
    tabs = jnp.asarray(tables(W))
    obj = object_slices.reshape(PLANES, TR, TC)
    top = positions[:, 0] - lax.axis_index("row") * TR
    left = positions[:, 1] - lax.axis_index("col") * TC
    place = jnp.stack([jnp.append(top, counts[0]), jnp.append(left, counts[0])], axis=1)
    ranges = list(zip(CUTS[1:], CUTS[:-1]))
    head, *pieces, total = first_pieces(obj, [(0, W)] + ranges[:AHEAD])
    rights = [(TR, shifted(head, (-1, -1)))]
    mine = [(TR, shifted(head, (-1, 0))), (0, obj)]
    carry = drop = None
    parts = []
    for at, (low, high) in enumerate(ranges):
        rights += [(ranges[len(rights) - 1 + i][0], shifted(piece, (0, -1))) for i, piece in enumerate(pieces)]
        send = ranges[at + AHEAD] if at + AHEAD < len(ranges) else None
        outs = list(
            range_gradients(low, high, place, probe, tabs, amplitude, drop, carry, mine, rights, send)
        )
        main, spill = outs[:2]
        pieces = [outs.pop()] if send else []
        carry = outs[2] if low > 0 else None
        if high == TR:
            drop = shifted(outs[3], (1, 0))
        begin = low + W if low > 0 else 0
        parts.append((begin, main, shifted(spill, (0, 1))))
    for begin, main, spill in parts:
        total = lax.dynamic_update_slice(total, main + spill.astype(F32), (0, begin, 0))
    return total.reshape(S, 2, TR, TC)


def solution(mesh):
    placed = (
        P(None, None, "row", "col"),
        P(),
        P(("row", "col"), None),
        P(("row", "col")),
        P(("row", "col"), None, None),
    )
    return jax.shard_map(
        body, mesh=mesh, in_specs=placed, out_specs=P(None, None, "row", "col"), check_vma=False
    )
```

```python
import functools
import math

import jax
import jax.numpy as jnp
import numpy as np
from jax import lax
from jax.experimental import pallas as pl
from jax.experimental.pallas import tpu as pltpu
from jax.sharding import PartitionSpec as P

W = 256
S = 2
SLOTS = 16
TR = 2048
TC = 256
PLANES = 2 * S
BF16 = jnp.bfloat16
F32 = jnp.float32
CUTS = (2048, 1664, 1408, 1088, 768, 448, 128, 0)
AHEAD = 3
GROUP = 16
LANES = 128


def shifted(value, moves):
    rows, cols = lax.axis_size("row"), lax.axis_size("col")
    pairs = [
        (r * cols + c, (r + moves[0]) * cols + c + moves[1])
        for r in range(rows)
        for c in range(cols)
        if 0 <= r + moves[0] < rows and 0 <= c + moves[1] < cols
    ]
    return lax.ppermute(value, ("row", "col"), pairs)


def tables(width):
    index = np.arange(width)
    four = np.exp(-2j * np.pi * (index[:, None] * index[None, :] % width) / width) / math.sqrt(width)
    freq = (index + width // 2) % width - width // 2
    prop = (four.conj() * np.exp(-1j * np.pi * freq * freq / (4.0 * width))) @ four
    forms = []
    for table in (prop, four):
        re, im = table.real.astype(np.float32), table.imag.astype(np.float32)
        forms.append(np.block([[re, -im], [im, re]]))
        forms.append(np.block([[re, im], [-im, re]]))
    return np.stack(forms).astype(BF16)


def transform(left, right, re, im):
    field = jnp.concatenate([re.astype(BF16), im.astype(BF16)], axis=0)
    half = jnp.dot(left, field, preferred_element_type=F32).astype(BF16)
    half = jnp.concatenate([half[:W], half[W:]], axis=1)
    out = jnp.dot(half, right, preferred_element_type=F32)
    return out[:, :W], out[:, W:]


def window_gradients(windows, amps, probes, tabs, emit):
    many = range(len(amps))
    q_l, q_r, f_l, f_r = (tabs[i] for i in range(4))
    entering, fars, backs, lasts = {}, {}, {}, {}

    def stage(i, k):
        p, w = probes[i], windows[i]
        if k == 0:
            entering[i] = transform(q_l, q_r, p[0] * w[0] - p[1] * w[1], p[0] * w[1] + p[1] * w[0])
        elif k == 1:
            e = entering[i]
            fars[i] = transform(f_l, f_r, e[0] * w[2] - e[1] * w[3], e[0] * w[3] + e[1] * w[2])
        elif k == 2:
            f = fars[i]
            factor = 1.0 - amps[i] * lax.rsqrt(f[0] * f[0] + f[1] * f[1] + 1.0)
            backs[i] = transform(f_r, f_l, f[0] * factor, f[1] * factor)
        elif k == 3:
            b, e = backs[i], entering[i]
            lasts[i] = transform(q_r, q_l, b[0] * w[2] + b[1] * w[3], b[1] * w[2] - b[0] * w[3])
            emit(i, 2, e[0] * b[0] + e[1] * b[1])
            emit(i, 3, e[0] * b[1] - e[1] * b[0])
        else:
            b = lasts[i]
            emit(i, 0, p[0] * b[0] + p[1] * b[1])
            emit(i, 1, p[0] * b[1] - p[1] * b[0])

    for k in range(5):
        for i in many:
            stage(i, k)


def range_kernel(low, high, mine_parts, right_parts, whole, send, *refs):
    refs = list(refs)
    span = high - low
    first, last = high == TR, low == 0
    take = refs.pop
    place_ref, probe_ref, tab_ref, amp_ref = (take(0) for _ in range(4))
    drop_ref = take(0) if last else None
    carry_ref = None if first else take(0)
    mine_refs = [take(0) for _ in range(1 + max(part[0] for part in mine_parts))]
    right_refs = [take(0) for _ in range(1 + max(part[0] for part in right_parts))]
    main_ref, spill_ref = take(0), take(0)
    next_ref = None if last else take(0)
    fall_ref = take(0) if first else None
    send_ref = take(0) if send else None
    mine, right, acc, amps, win, gone, order, amp_sem, sem = refs

    copies = []
    for parts, sources, target in ((mine_parts, mine_refs, mine), (right_parts, right_refs, right)):
        for which, start, at, rows in parts:
            copies.append((sources[which].at[:, pl.ds(start, rows)], target.at[:, pl.ds(at, rows)]))
    if not first:
        copies.append((carry_ref, acc.at[:, pl.ds(span, W)]))
    copies = [pltpu.make_async_copy(a, b, sem.at[i]) for i, (a, b) in enumerate(copies)]
    for copy in copies:
        copy.start()
    if send:
        ahead = pltpu.make_async_copy(mine_refs[whole].at[:, pl.ds(send[0], send[1] - send[0])], send_ref, sem.at[7])
        ahead.start()

    def amp_copy(slot):
        return pltpu.make_async_copy(amp_ref.at[slot], amps.at[slot], amp_sem.at[slot])

    count = jnp.zeros((), jnp.int32)
    inside = []
    for slot in range(SLOTS):
        top = place_ref[slot, 0]
        here = jnp.logical_and(slot < place_ref[SLOTS, 0], jnp.logical_and(top >= low, top < high))
        inside.append(here)

        @pl.when(here)
        def _(slot=slot, count=count):
            order[count] = slot
            amp_copy(slot).start()

        count = count + here.astype(jnp.int32)

    fresh = span + W if first else span
    acc[:, :fresh] = jnp.zeros((PLANES, fresh, 2 * TC), F32)
    for copy in copies:
        copy.wait()
    if last:
        acc[:, :W] += drop_ref[...].astype(F32)
    for slot in range(SLOTS):

        @pl.when(inside[slot])
        def _(slot=slot):
            amp_copy(slot).wait()

    row = lax.broadcasted_iota(jnp.int32, (GROUP, TC), 0)
    col = lax.broadcasted_iota(jnp.int32, (GROUP, TC), 1)
    row_b, col_b = row.astype(F32).astype(BF16), col.astype(F32).astype(BF16)
    groups = range(W // GROUP)

    def step(start, width):
        slots, places, windows, probes = [], [], [], []
        for which in range(width):
            slot = order[start + which]
            top = place_ref[slot, 0] - low
            base = top // W * W
            turn = top - base
            edge = place_ref[slot, 1]
            split = turn // GROUP
            rest = turn - split * GROUP
            beside = col_b >= jnp.full((GROUP, TC), edge, jnp.int32).astype(F32).astype(BF16)
            rows = [pl.multiple_of(base + GROUP * i + jnp.where(i < split, W, 0), GROUP) for i in groups]
            near = pl.ds(pl.multiple_of(base + GROUP * split, GROUP), GROUP)
            far = pl.ds(pl.multiple_of(base + GROUP * split + W, GROUP), GROUP)
            cut = pl.ds(pl.multiple_of(GROUP * split, GROUP), GROUP)
            below = row_b >= jnp.full((GROUP, TC), rest, jnp.int32).astype(F32).astype(BF16)
            for plane in range(PLANES):
                for i in groups:
                    part = pl.ds(rows[i], GROUP)
                    win[which, plane, GROUP * i : GROUP * (i + 1)] = jnp.where(
                        beside, mine[plane, part], right[plane, part]
                    )
                one = jnp.where(below, mine[plane, near], mine[plane, far])
                two = jnp.where(below, right[plane, near], right[plane, far])
                win[which, plane, cut] = jnp.where(beside, one, two)
            turned = [
                jnp.concatenate([probe_ref[part, half, pl.ds(W - turn, W)] for half in range(TC // LANES)], axis=1)
                for part in range(2)
            ]
            probes.append([pltpu.roll(part, edge, 1) for part in turned])
            windows.append([win[which, plane].astype(F32) for plane in range(PLANES)])
            slots.append(slot)
            places.append((split, rest, col >= edge, rows, far, cut))

        def emit(which, plane, grad):
            split, rest, beside, rows, far, cut = places[which]
            gone[which, plane] = grad
            for i in groups:
                first_row = jnp.where(i == split, rest, 0)
                part = grad[GROUP * i : GROUP * (i + 1)]
                part = jnp.where(row >= first_row, part, 0.0)
                left = jnp.where(beside, part, 0.0)
                acc[plane, pl.ds(rows[i], GROUP), :TC] += left
                acc[plane, pl.ds(rows[i], GROUP), TC:] += part - left
            part = jnp.where(row < rest, gone[which, plane, cut], 0.0)
            left = jnp.where(beside, part, 0.0)
            acc[plane, far, :TC] += left
            acc[plane, far, TC:] += part - left

        window_gradients(windows, [amps[s].astype(F32) for s in slots], probes, tab_ref, emit)

    pl.loop(0, count // 2)(lambda pair: step(2 * pair, 2))
    pl.when(count % 2 == 1)(lambda: step(count - 1, 1))
    begin = 0 if last else W
    end = span if first else span + W
    results = [(acc.at[:, pl.ds(begin, end - begin), pl.ds(0, TC)], main_ref)]
    if not last:
        results.append((acc.at[:, pl.ds(0, W)], next_ref))
    results = [pltpu.make_async_copy(a, b, sem.at[i]) for i, (a, b) in enumerate(results)]
    for copy in results:
        copy.start()
    spill_ref[...] = acc[:, begin:end, TC:].astype(BF16)
    if first:
        fall_ref[...] = acc[:, span : span + W].astype(BF16)
    for copy in results:
        copy.wait()
    if send:
        ahead.wait()


def parts_of(low, high, pieces):
    used = [i for i, (a, b) in enumerate(pieces) if max(a, low) < min(b, high)]
    parts = []
    for which, i in enumerate(used):
        a, b = max(pieces[i][0], low), min(pieces[i][1], high)
        parts.append((which, a - pieces[i][0], a - low, b - a))
    return used, parts


def range_gradients(low, high, place, probe, tabs, amplitude, drop, carry, mine, rights, send):
    span = high - low
    first, last = high == TR, low == 0
    top = -(-span // W) * W + W
    spans = [[(at, at + array.shape[1]) for at, array in side] for side in (mine, rights)]
    mine_used, mine_parts = parts_of(low, high + W, spans[0])
    right_used, right_parts = parts_of(low, high + W, spans[1])
    anywhere = pl.BlockSpec(memory_space=pl.ANY)
    vmem = pl.BlockSpec(memory_space=pltpu.VMEM)
    args = [(place, pl.BlockSpec(memory_space=pltpu.SMEM)), (probe, vmem), (tabs, vmem), (amplitude, pl.BlockSpec(memory_space=pltpu.HBM))]
    if last:
        args.append((drop, vmem))
    if not first:
        args.append((carry, anywhere))
    args += [(mine[i][1], anywhere) for i in mine_used]
    args += [(rights[i][1], anywhere) for i in right_used]
    final = span + W * (int(last) - int(first))
    outs = [((PLANES, final, TC), F32, anywhere), ((PLANES, final, TC), BF16, vmem)]
    if not last:
        outs.append(((PLANES, W, 2 * TC), F32, anywhere))
    if first:
        outs.append(((PLANES, W, 2 * TC), BF16, vmem))
    if send:
        outs.append(((PLANES, send[1] - send[0], TC), BF16, vmem))
    whole = mine_used.index(len(mine) - 1)
    return pl.pallas_call(
        functools.partial(range_kernel, low, high, mine_parts, right_parts, whole, send),
        out_shape=[jax.ShapeDtypeStruct(shape, kind) for shape, kind, _ in outs],
        in_specs=[spec for _, spec in args],
        out_specs=[spec for _, _, spec in outs],
        scratch_shapes=[
            pltpu.VMEM((PLANES, top, TC), BF16),
            pltpu.VMEM((PLANES, top, TC), BF16),
            pltpu.VMEM((PLANES, top, 2 * TC), F32),
            pltpu.VMEM((SLOTS, W, W), BF16),
            pltpu.VMEM((2, PLANES, W, W), BF16),
            pltpu.VMEM((2, PLANES, W, W), F32),
            pltpu.SMEM((SLOTS,), jnp.int32),
            pltpu.SemaphoreType.DMA((SLOTS,)),
            pltpu.SemaphoreType.DMA((8,)),
        ],
        compiler_params=pltpu.CompilerParams(vmem_limit_bytes=40 << 20),
        cost_estimate=pl.CostEstimate(flops=3 << 30, bytes_accessed=12 << 20, transcendentals=1 << 17),
    )(*[array for array, _ in args])


def first_pieces(obj, rows):
    def kernel(obj_ref, *refs):
        sem = refs[-1]
        copies = [
            pltpu.make_async_copy(obj_ref.at[:, pl.ds(low, high - low)], ref, sem.at[i])
            for i, ((low, high), ref) in enumerate(zip(rows, refs))
        ]
        for copy in copies:
            copy.start()
        for copy in copies:
            copy.wait()

    anywhere = pl.BlockSpec(memory_space=pl.ANY)
    return pl.pallas_call(
        kernel,
        out_shape=[jax.ShapeDtypeStruct((PLANES, high - low, TC), BF16) for low, high in rows]
        + [jax.ShapeDtypeStruct((PLANES, TR, TC), F32)],
        in_specs=[anywhere],
        out_specs=[pl.BlockSpec(memory_space=pltpu.VMEM)] * len(rows) + [pl.BlockSpec(memory_space=pltpu.HBM)],
        scratch_shapes=[pltpu.SemaphoreType.DMA((len(rows),))],
        cost_estimate=pl.CostEstimate(flops=0, bytes_accessed=4 << 20, transcendentals=0),
    )(obj)


def body(object_slices, probe, positions, counts, amplitude):
    tabs = jnp.asarray(tables(W))
    obj = object_slices.reshape(PLANES, TR, TC)
    probe = jnp.concatenate([probe, probe], axis=1).reshape(2, 2 * W, TC // LANES, LANES).transpose(0, 2, 1, 3)
    top = positions[:, 0] - lax.axis_index("row") * TR
    left = positions[:, 1] - lax.axis_index("col") * TC
    place = jnp.stack([jnp.append(top, counts[0]), jnp.append(left, counts[0])], axis=1)
    ranges = list(zip(CUTS[1:], CUTS[:-1]))
    head, *pieces, total = first_pieces(obj, [(0, W)] + ranges[:AHEAD])
    rights = [(TR, shifted(head, (-1, -1)))]
    mine = [(TR, shifted(head, (-1, 0))), (0, obj)]
    carry = drop = None
    parts = []
    for at, (low, high) in enumerate(ranges):
        rights += [(ranges[len(rights) - 1 + i][0], shifted(piece, (0, -1))) for i, piece in enumerate(pieces)]
        send = ranges[at + AHEAD] if at + AHEAD < len(ranges) else None
        outs = list(
            range_gradients(low, high, place, probe, tabs, amplitude, drop, carry, mine, rights, send)
        )
        main, spill = outs[:2]
        pieces = [outs.pop()] if send else []
        carry = outs[2] if low > 0 else None
        if high == TR:
            drop = shifted(outs[3], (1, 0))
        begin = low + W if low > 0 else 0
        parts.append((begin, main, shifted(spill, (0, 1))))
    for begin, main, spill in parts:
        total = lax.dynamic_update_slice(total, main + spill.astype(F32), (0, begin, 0))
    return total.reshape(S, 2, TR, TC)


def solution(mesh):
    placed = (
        P(None, None, "row", "col"),
        P(),
        P(("row", "col"), None),
        P(("row", "col")),
        P(("row", "col"), None, None),
    )
    return jax.shard_map(
        body, mesh=mesh, in_specs=placed, out_specs=P(None, None, "row", "col"), check_vma=False
    )
```
